512 devices in a mesh: occ: 64 (over z_lo, y, core), aux: 8 (over z_hi, x).
Axes of the slice: x: 4, y: 8, z: 8 (z_hi: 2, z_lo: 4; z = z_hi * 4 + z_lo), core: 2. Of those that a mesh axis runs over, the one named last changes fastest.
Arguments:
- ints_b: bfloat16 [64, 1024, 5120], P('occ', None, 'aux'), may hold values from -0.69921875 to 0.69921875
- occ_energy: float32 [64], P('occ'), may hold values from -2 to -0.4
- virt_energy: float32 [1024], replicated, may hold values from 0.2 to 3
Outputs:
- gamma_grad: float32 [64, 1024, 5120], P('occ', None, 'aux')
The draws below stay inside these ranges and needn't reach their ends.
All inputs are finite; a program needn't handle non-finite values.
Results may differ from the reference program's by a relative error of at most 0.015.
Values may be sent and summed in bfloat16 or wider, within the bound.
A program may use at most 64 MiB of HBM per device.

```python
import math
import jax
import jax.numpy as jnp
from jax import lax

OCC_DEV = 1
VIRT = 1024
NAUX = 5120
OCC = 64
N_OCC = 64
N_AUX = 8


def block_levels(own_key, shape, cuts, low, high):
    loudness, own = 1.0, jax.random.fold_in(own_key, 6)
    for axis_at, blocks in cuts:
        draws = jnp.exp(jax.random.uniform(jax.random.fold_in(own, axis_at), (blocks,), jnp.float32, low / len(cuts), high / len(cuts)))
        loudness = loudness * jnp.repeat(draws, shape[axis_at] // blocks).reshape([-1 if axis == axis_at else 1 for axis in range(len(shape))])
    return loudness


def centred(own_key, extent, spread, limit, cuts=(), held_as=jnp.bfloat16):
    entries = spread * jax.random.normal(own_key, extent, jnp.float32)
    if cuts:
        entries = entries * block_levels(own_key, extent, cuts, -0.22, 0.18)
    return jnp.clip(entries, -limit, limit).astype(held_as)


def setup_inputs(seed: int = 0) -> dict:
    arg_keys = jax.random.split(jax.random.key(seed), 4)
    return {
        "ints_b": centred(arg_keys[0], (OCC, VIRT, NAUX), 0.1192, 0.69921875, ((0, 64), (2, 8))),
        "occ_energy": jnp.clip(-2.0 + 1.6 * jax.random.uniform(arg_keys[1], (OCC,), jnp.float32) ** block_levels(arg_keys[1], (OCC,), ((0, 64),), -0.2, 0.2), -2.0, -0.4),
        "virt_energy": jnp.clip(jnp.exp(jax.random.uniform(arg_keys[2], (VIRT,), jnp.float32, math.log(0.2), math.log(3.0))), 0.2, 3.0),
    }


def reference(ints_b, occ_energy, virt_energy):
    per = NAUX // N_AUX
    blocks = ints_b.reshape(N_OCC, OCC_DEV, VIRT, NAUX)
    eblocks = occ_energy.reshape(N_OCC, OCC_DEV)

    def one_block(index):
        mine = lax.dynamic_index_in_dim(blocks, index, 0, keepdims=False)
        emine = lax.dynamic_index_in_dim(eblocks, index, 0, keepdims=False)
        mine_f = mine.astype(jnp.float32)
        mine_g = mine_f.reshape(OCC_DEV, VIRT, N_AUX, per).transpose(2, 0, 1, 3)
        total = jnp.zeros((OCC_DEV, VIRT, NAUX), jnp.float32)
        for offset in (1, -1):
            other_index = ((index + offset + N_OCC) % N_OCC).astype(jnp.int32)
            other = lax.dynamic_index_in_dim(blocks, other_index, 0, keepdims=False)
            eother = lax.dynamic_index_in_dim(eblocks, other_index, 0, keepdims=False)
            other_f = other.astype(jnp.float32)
            other_g = other_f.reshape(OCC_DEV, VIRT, N_AUX, per).transpose(2, 0, 1, 3)

            def group(carry, pieces):
                partial_value = jnp.einsum('iap,jbp->ijab', pieces[0], pieces[1])
                rounded = lax.optimization_barrier(partial_value.astype(jnp.bfloat16))
                return carry + rounded.astype(jnp.float32), None

            start = jnp.zeros((OCC_DEV, OCC_DEV, VIRT, VIRT), jnp.float32)
            coulomb, _ = lax.scan(group, start, (mine_g, other_g))
            denom = (emine[:, None, None, None] + eother[None, :, None, None]
                     - virt_energy[None, None, :, None] - virt_energy[None, None, None, :])
            amplitude = (coulomb / denom).astype(jnp.bfloat16)
            total = total + jnp.einsum('ijab,jbp->iap', amplitude.astype(jnp.float32), other_f)
        return total

    result = lax.map(one_block, jnp.arange(N_OCC, dtype=jnp.int32))
    return result.reshape(OCC_DEV * N_OCC, VIRT, NAUX)
```

```python
import functools

import jax
import jax.numpy as jnp
from jax import lax
from jax.experimental import pallas as pl
from jax.experimental.pallas import tpu as pltpu
from jax.sharding import PartitionSpec as P

MESH = pl.DeviceIdType.MESH
NX = 4
PLANE = 16
STEPS = (64, 64, 64, 64)
RELAYED = (1, 3)
ORDER = ('p0', 'p1', 'r0', 'h1', 'p2', 'r1', 'z0', 'h3', 'p3', 'r2', 'z1', 'r3', 'z2', 'z3', 'a0', 'a1', 'f0', 'a2', 'f1', 'g0', 'a3', 'f2', 'g1', 'f3', 'g2', 'g3')
KINDS = (
    "b", "e", "hop", "relay_r", "relay_l", "direct_r", "direct_l", "sum_r", "sum_l", "z", "ag_r", "ag_l", "fw_r", "fw_l", "ret"
)


def kernel(
    ints_ref, energy_ref, virt_hbm, acc, ret_out,
    mine, left_b, hop, virt_ref, part, relay_l, relay_r, direct_l, direct_r, sum_l, sum_r,
    zsend, zrecv, amp, inverse, esend, erecv, ret_send,
    send_sem, recv_sem, local_sem, late_sem,
):
    occ, aux = lax.axis_index("occ"), lax.axis_index("aux")
    n_occ = lax.axis_size("occ")
    x, zh = lax.rem(aux, NX), aux // NX
    xr, xl, xo = lax.rem(x + 1, NX), lax.rem(x + NX - 1, NX), lax.rem(x + 2, NX)
    right, left = (occ, zh * NX + xr), (occ, zh * NX + xl)
    partner = (occ, (1 - zh) * NX + x)
    above, below = (lax.rem(occ + 1, n_occ), aux), (lax.rem(occ + n_occ - 1, n_occ), aux)
    offsets = [sum(STEPS[:s]) for s in range(len(STEPS))]

    load = pltpu.make_async_copy(ints_ref, mine, local_sem.at[0])
    load.start()
    load_virt = pltpu.make_async_copy(virt_hbm, virt_ref, local_sem.at[1])
    load_virt.start()
    energy = energy_ref[0]
    esend[...] = jnp.full(esend.shape, energy, jnp.float32)

    place = lax.rem(occ, PLANE)
    top = place // (PLANE - 1)
    bottom = 1 - (place + PLANE - 1) // PLANE
    next_top = (lax.rem(occ + PLANE, n_occ), aux)
    last_top = (lax.rem(occ + n_occ - PLANE, n_occ), aux)
    first_here = (lax.rem(occ + n_occ - PLANE + 1, n_occ), aux)
    top_here = (lax.rem(occ + PLANE - 1, n_occ), aux)

    def greet(device):
        pl.semaphore_signal(barrier, inc=1, device_id=device, device_id_type=MESH)

    barrier = pltpu.get_barrier_semaphore()
    for device in (right, left, above, below):
        greet(device)

    @pl.when(zh == 0)
    def _():
        greet(partner)

    @pl.when(top == 1)
    def _():
        greet(next_top)
        greet(last_top)
        greet(first_here)

    @pl.when(bottom == 1)
    def _():
        greet(top_here)

    pl.semaphore_wait(barrier, 4 + zh + 3 * top + bottom)

    @pl.when(zh == 1)
    def _():
        pl.semaphore_signal(late_sem, inc=1, device_id=partner, device_id_type=MESH)

    load.wait()

    started = []

    def copy(kind, s, src, dst, device):
        at = KINDS.index(kind)
        return pltpu.make_async_remote_copy(
            src_ref=src, dst_ref=dst, send_sem=send_sem.at[at, s], recv_sem=recv_sem.at[at, s],
            device_id=device, device_id_type=MESH,
        )

    def send(kind, s, src, dst, device, only=None):
        one = copy(kind, s, src, dst, device)
        if only is None:
            one.start()
        else:
            pl.when(only)(one.start)
        started.append((one, only))

    def arrive(kind, s, dst, device):
        copy(kind, s, dst, dst, device).wait_recv()

    def rows(s):
        return pl.ds(offsets[s], STEPS[s])

    def half(s, h):
        return pl.ds(offsets[s] + h * STEPS[s] // 2, STEPS[s] // 2)

    def f32(value):
        return value.astype(jnp.float32)

    send("e", 0, esend, erecv, above)
    for s in range(len(STEPS)):
        if s in RELAYED:
            send("b", s, mine.at[:, rows(s), :], left_b.at[:, rows(s), :], above, top == 0)
            send("hop", s, mine.at[:, rows(s), :], hop.at[:, rows(s), :], next_top, top == 1)
        else:
            send("b", s, mine.at[:, rows(s), :], left_b.at[:, rows(s), :], above)
    load_virt.wait()

    def prepare():
        arrive("e", 0, erecv, below)
        quarter = amp.shape[1]
        column = jnp.broadcast_to(
            virt_ref[0:1, pl.ds(pl.multiple_of(x * quarter, quarter), quarter)], (128, quarter)
        ).T
        row = erecv[0:1, :] + energy - virt_ref[0:1, :]
        inverse[...] = 1.0 / (row - column[:, 0:1])

    def h(s):
        @pl.when(top == 1)
        def _():
            arrive("hop", s, hop.at[:, rows(s), :], last_top)

        send("b", s, hop.at[:, rows(s), :], left_b.at[:, rows(s), :], first_here, top == 1)

    def p(s):
        arrive("b", s, left_b.at[:, rows(s), :], below)
        theirs = left_b[:, rows(s), :].reshape(NX * STEPS[s], -1)
        value = lax.dot_general(
            theirs, mine[...].reshape(-1, mine.shape[-1]), (((1,), (1,)), ((), ())), preferred_element_type=jnp.float32
        )
        part[:, rows(s), :] = value.astype(jnp.bfloat16).reshape(NX, STEPS[s], -1)
        send("relay_r", s, part.at[xo, half(s, 0)], relay_l.at[half(s, 0)], right)
        send("relay_l", s, part.at[xo, half(s, 1)], relay_r.at[half(s, 1)], left)
        send("direct_r", s, part.at[xr, half(s, 1)], direct_l.at[half(s, 1)], right)
        send("direct_l", s, part.at[xl, half(s, 0)], direct_r.at[half(s, 0)], left)

    def r(s):
        arrive("relay_r", s, relay_l.at[half(s, 0)], left)
        relay_l[half(s, 0), :] = (f32(relay_l[half(s, 0), :]) + f32(part[xr, half(s, 0), :])).astype(jnp.bfloat16)
        send("sum_r", s, relay_l.at[half(s, 0)], sum_l.at[half(s, 0)], right)
        arrive("relay_l", s, relay_r.at[half(s, 1)], right)
        relay_r[half(s, 1), :] = (f32(relay_r[half(s, 1), :]) + f32(part[xl, half(s, 1), :])).astype(jnp.bfloat16)
        send("sum_l", s, relay_r.at[half(s, 1)], sum_r.at[half(s, 1)], left)

    def z(s):
        arrive("direct_l", s, direct_r.at[half(s, 0)], right)
        arrive("sum_r", s, sum_l.at[half(s, 0)], left)
        zsend[half(s, 0), :] = (
            f32(part[x, half(s, 0), :]) + f32(sum_l[half(s, 0), :]) + f32(direct_r[half(s, 0), :])
        ).astype(jnp.bfloat16)
        arrive("direct_r", s, direct_l.at[half(s, 1)], left)
        arrive("sum_l", s, sum_r.at[half(s, 1)], right)
        zsend[half(s, 1), :] = (
            f32(part[x, half(s, 1), :]) + f32(sum_r[half(s, 1), :]) + f32(direct_l[half(s, 1), :])
        ).astype(jnp.bfloat16)
        if s == 0:

            @pl.when(zh == 0)
            def _():
                pl.semaphore_wait(late_sem, 1)

        send("z", s, zsend.at[rows(s)], zrecv.at[rows(s)], partner)

    def a(s):
        if s == 0:
            prepare()
        arrive("z", s, zrecv.at[rows(s)], partner)
        coulomb = f32(zsend[rows(s), :]) + f32(zrecv[rows(s), :])
        amp[x, rows(s), :] = (coulomb * inverse[rows(s), :]).astype(jnp.bfloat16)
        send("ag_r", s, amp.at[x, rows(s)], amp.at[x, rows(s)], right)
        send("ag_l", s, amp.at[x, rows(s)], amp.at[x, rows(s)], left)

    def f(s):
        arrive("ag_r", s, amp.at[xl, rows(s)], left)
        send("fw_r", s, amp.at[xl, half(s, 0)], amp.at[xl, half(s, 0)], right)
        arrive("ag_l", s, amp.at[xr, rows(s)], right)
        send("fw_l", s, amp.at[xr, half(s, 1)], amp.at[xr, half(s, 1)], left)

    def g(s):
        arrive("fw_r", s, amp.at[xo, half(s, 0)], left)
        arrive("fw_l", s, amp.at[xo, half(s, 1)], right)
        block = amp[:, rows(s), :].reshape(NX * STEPS[s], -1)
        back = jnp.dot(block, mine[...].reshape(-1, mine.shape[-1]), preferred_element_type=jnp.float32)
        ret_send[:, rows(s), :] = back.astype(jnp.bfloat16).reshape(NX, STEPS[s], -1)
        send("ret", s, ret_send.at[:, rows(s), :], ret_out.at[:, rows(s), :], below)
        theirs = left_b[:, rows(s), :].reshape(NX * STEPS[s], -1)
        own = lax.dot_general(block, theirs, (((0,), (0,)), ((), ())), preferred_element_type=jnp.float32)
        if s == 0:
            acc[...] = own
        else:
            acc[...] += own

    act = {"h": h, "p": p, "r": r, "z": z, "a": a, "f": f, "g": g}
    for item in ORDER:
        act[item[0]](int(item[1:]))

    for s in range(len(STEPS)):
        arrive("ret", s, ret_out.at[:, rows(s), :], above)
    for one, only in started:
        if only is None:
            one.wait_send()
        else:
            pl.when(only)(one.wait_send)


def per_device(ints_b, occ_energy, virt_energy):
    _, virt, naux = ints_b.shape
    quarter = virt // NX
    bf16, f32 = jnp.bfloat16, jnp.float32
    steps = len(STEPS)
    hbm, vmem = pl.BlockSpec(memory_space=pltpu.HBM), pl.BlockSpec(memory_space=pltpu.VMEM)
    slab = pltpu.VMEM((quarter, virt), bf16)
    kept, returned = pl.pallas_call(
        kernel,
        out_shape=(jax.ShapeDtypeStruct((virt, naux), f32), jax.ShapeDtypeStruct((NX, quarter, naux), bf16)),
        in_specs=[hbm, pl.BlockSpec(memory_space=pltpu.SMEM), hbm],
        out_specs=(vmem, vmem),
        scratch_shapes=[
            pltpu.VMEM((NX, quarter, naux), bf16),
            pltpu.VMEM((NX, quarter, naux), bf16),
            pltpu.VMEM((NX, quarter, naux), bf16),
            pltpu.VMEM((1, virt), f32),
            pltpu.VMEM((NX, quarter, virt), bf16),
            slab, slab, slab, slab, slab, slab,
            slab, slab,
            pltpu.VMEM((NX, quarter, virt), bf16),
            pltpu.VMEM((quarter, virt), f32),
            pltpu.VMEM((8, virt), f32),
            pltpu.VMEM((8, virt), f32),
            pltpu.VMEM((NX, quarter, naux), bf16),
            pltpu.SemaphoreType.DMA((len(KINDS), steps)),
            pltpu.SemaphoreType.DMA((len(KINDS), steps)),
            pltpu.SemaphoreType.DMA((2,)),
            pltpu.SemaphoreType.REGULAR,
        ],
        compiler_params=pltpu.CompilerParams(collective_id=0, has_side_effects=True, vmem_limit_bytes=48 * 2**20),
        cost_estimate=pl.CostEstimate(flops=6 * virt * virt * naux, bytes_accessed=10 * virt * naux, transcendentals=0),
        name="pair_gradient",
    )(ints_b.reshape(NX, quarter, naux), occ_energy, virt_energy.reshape(1, virt))
    total = kept + returned.reshape(virt, naux).astype(f32)
    return total.reshape(1, virt, naux)


def solution(mesh):
    placed = (P("occ", None, "aux"), P("occ"), P())
    return jax.shard_map(
        per_device, mesh=mesh, in_specs=placed, out_specs=P("occ", None, "aux"), check_vma=False
    )
```

```python
import functools

import jax
import jax.numpy as jnp
from jax import lax
from jax.experimental import pallas as pl
from jax.experimental.pallas import tpu as pltpu
from jax.sharding import PartitionSpec as P

MESH = pl.DeviceIdType.MESH
ADD_PIECES = 4
NX = 4
PLANE = 16
STEPS = (64, 64, 64, 32, 32)
RELAYED = (1, 2, 4)
ORDER = ('p0', 'p1', 'r0', 'h1', 'p2', 'r1', 'z0', 'h2', 'p3', 'r2', 'z1', 'h4', 'p4', 'r3', 'z2', 'r4', 'z3', 'z4', 'a0', 'a1', 'f0', 'a2', 'f1', 'g0', 'a3', 'f2', 'g1', 'a4', 'f3', 'g2', 'f4', 'g3', 'k4', 'g4', 'q0')
KINDS = (
    "b", "e", "hop", "relay_r", "relay_l", "direct_r", "direct_l", "sum_r", "sum_l", "z", "ag_r", "ag_l", "fw_r", "fw_l", "ret",
    "ret_own", "ret_l", "ret_r",
)


def kernel(
    ints_ref, energy_ref, virt_hbm, acc_out, ret_out,
    mine, left_b, hop, virt_ref, part, relay_l, relay_r, direct_l, direct_r, sum_l, sum_r,
    zsend, zrecv, amp, inverse, esend, erecv, ret_send, acc,
    send_sem, recv_sem, local_sem, late_sem,
):
    occ, aux = lax.axis_index("occ"), lax.axis_index("aux")
    n_occ = lax.axis_size("occ")
    x, zh = lax.rem(aux, NX), aux // NX
    xr, xl, xo = lax.rem(x + 1, NX), lax.rem(x + NX - 1, NX), lax.rem(x + 2, NX)
    right, left = (occ, zh * NX + xr), (occ, zh * NX + xl)
    partner = (occ, (1 - zh) * NX + x)
    above, below = (lax.rem(occ + 1, n_occ), aux), (lax.rem(occ + n_occ - 1, n_occ), aux)
    offsets = [sum(STEPS[:s]) for s in range(len(STEPS))]

    load = pltpu.make_async_copy(ints_ref, mine, local_sem.at[0])
    load.start()
    load_virt = pltpu.make_async_copy(virt_hbm, virt_ref, local_sem.at[1])
    load_virt.start()
    energy = energy_ref[0]
    esend[...] = jnp.full(esend.shape, energy, jnp.float32)

    place = lax.rem(occ, PLANE)
    top = place // (PLANE - 1)
    bottom = 1 - (place + PLANE - 1) // PLANE
    next_top = (lax.rem(occ + PLANE, n_occ), aux)
    last_top = (lax.rem(occ + n_occ - PLANE, n_occ), aux)
    first_here = (lax.rem(occ + n_occ - PLANE + 1, n_occ), aux)
    top_here = (lax.rem(occ + PLANE - 1, n_occ), aux)

    is_top, not_top = top == 1, top == 0

    def greet(device):
        pl.semaphore_signal(barrier, inc=1, device_id=device, device_id_type=MESH)

    barrier = pltpu.get_barrier_semaphore()
    for device in (right, left, above, below):
        greet(device)

    @pl.when(zh == 0)
    def _():
        greet(partner)

    @pl.when(is_top)
    def _():
        greet(next_top)
        greet(last_top)
        greet(first_here)

    @pl.when(bottom == 1)
    def _():
        greet(top_here)

    pl.semaphore_wait(barrier, 4 + zh + 3 * top + bottom)

    @pl.when(zh == 1)
    def _():
        pl.semaphore_signal(late_sem, inc=1, device_id=partner, device_id_type=MESH)

    load.wait()

    started = {}
    first = {}

    def copy(kind, s, src, dst, device):
        at = KINDS.index(kind)
        return pltpu.make_async_remote_copy(
            src_ref=src, dst_ref=dst, send_sem=send_sem.at[at, s], recv_sem=recv_sem.at[at, s],
            device_id=device, device_id_type=MESH,
        )

    def send(kind, s, src, dst, device, only=None):
        one = copy(kind, s, src, dst, device)
        if only is None:
            one.start()
        else:
            pl.when(only)(one.start)
        started[kind, s, only is is_top] = (src, dst, device, only)

    def arrive(kind, s, dst, device):
        copy(kind, s, dst, dst, device).wait_recv()

    def rows(s):
        return pl.ds(offsets[s], STEPS[s])

    def half(s, h):
        return pl.ds(offsets[s] + h * STEPS[s] // 2, STEPS[s] // 2)

    def f32(value):
        return value.astype(jnp.float32)

    send("e", 0, esend, erecv, above)
    for s in range(len(STEPS)):
        if s in RELAYED:
            send("b", s, mine.at[:, rows(s), :], left_b.at[:, rows(s), :], above, not_top)
            send("hop", s, mine.at[:, rows(s), :], hop.at[:, rows(s), :], next_top, is_top)
        else:
            send("b", s, mine.at[:, rows(s), :], left_b.at[:, rows(s), :], above)
    load_virt.wait()

    def prepare():
        arrive("e", 0, erecv, below)
        quarter = amp.shape[1]
        column = jnp.broadcast_to(
            virt_ref[0:1, pl.ds(pl.multiple_of(x * quarter, quarter), quarter)], (128, quarter)
        ).T
        row = erecv[0:1, :] + energy - virt_ref[0:1, :]
        inverse[...] = 1.0 / (row - column[:, 0:1])

    def h(s):
        @pl.when(is_top)
        def _():
            arrive("hop", s, hop.at[:, rows(s), :], last_top)

        send("b", s, hop.at[:, rows(s), :], left_b.at[:, rows(s), :], first_here, is_top)

    def p(s):
        arrive("b", s, left_b.at[:, rows(s), :], below)
        theirs = left_b[:, rows(s), :].reshape(NX * STEPS[s], -1)
        value = lax.dot_general(
            theirs, mine[...].reshape(-1, mine.shape[-1]), (((1,), (1,)), ((), ())), preferred_element_type=jnp.float32
        )
        part[:, rows(s), :] = value.astype(jnp.bfloat16).reshape(NX, STEPS[s], -1)
        send("relay_r", s, part.at[xo, half(s, 0)], relay_l.at[half(s, 0)], right)
        send("relay_l", s, part.at[xo, half(s, 1)], relay_r.at[half(s, 1)], left)
        send("direct_r", s, part.at[xr, half(s, 1)], direct_l.at[half(s, 1)], right)
        send("direct_l", s, part.at[xl, half(s, 0)], direct_r.at[half(s, 0)], left)

    def r(s):
        arrive("relay_r", s, relay_l.at[half(s, 0)], left)
        relay_l[half(s, 0), :] = (f32(relay_l[half(s, 0), :]) + f32(part[xr, half(s, 0), :])).astype(jnp.bfloat16)
        send("sum_r", s, relay_l.at[half(s, 0)], sum_l.at[half(s, 0)], right)
        arrive("relay_l", s, relay_r.at[half(s, 1)], right)
        relay_r[half(s, 1), :] = (f32(relay_r[half(s, 1), :]) + f32(part[xl, half(s, 1), :])).astype(jnp.bfloat16)
        send("sum_l", s, relay_r.at[half(s, 1)], sum_r.at[half(s, 1)], left)

    def sum_halves(s):
        arrive("direct_l", s, direct_r.at[half(s, 0)], right)
        arrive("sum_r", s, sum_l.at[half(s, 0)], left)
        zsend[half(s, 0), :] = (
            f32(part[x, half(s, 0), :]) + f32(sum_l[half(s, 0), :]) + f32(direct_r[half(s, 0), :])
        ).astype(jnp.bfloat16)
        arrive("direct_r", s, direct_l.at[half(s, 1)], left)
        arrive("sum_l", s, sum_r.at[half(s, 1)], right)
        zsend[half(s, 1), :] = (
            f32(part[x, half(s, 1), :]) + f32(sum_r[half(s, 1), :]) + f32(direct_l[half(s, 1), :])
        ).astype(jnp.bfloat16)

    def z(s):
        sum_halves(s)
        if s == first["z"]:

            @pl.when(zh == 0)
            def _():
                pl.semaphore_wait(late_sem, 1)

        send("z", s, zsend.at[rows(s)], zrecv.at[rows(s)], partner)

    def a(s):
        if s == first["a"]:
            prepare()
        arrive("z", s, zrecv.at[rows(s)], partner)
        coulomb = f32(zsend[rows(s), :]) + f32(zrecv[rows(s), :])
        amp[x, rows(s), :] = (coulomb * inverse[rows(s), :]).astype(jnp.bfloat16)
        send("ag_r", s, amp.at[x, rows(s)], amp.at[x, rows(s)], right)
        send("ag_l", s, amp.at[x, rows(s)], amp.at[x, rows(s)], left)

    def f(s):
        arrive("ag_r", s, amp.at[xl, rows(s)], left)
        send("fw_r", s, amp.at[xl, half(s, 0)], amp.at[xl, half(s, 0)], right)
        arrive("ag_l", s, amp.at[xr, rows(s)], right)
        send("fw_l", s, amp.at[xr, half(s, 1)], amp.at[xr, half(s, 1)], left)

    split = [int(item[1:]) for item in ORDER if item[0] == "k"]
    quarters = (("ret_own", x), ("ret_l", xl), ("ret_r", xr), ("ret", xo))

    def give_back(kind, s, at):
        back = jnp.dot(amp[at, rows(s), :], mine[...].reshape(-1, mine.shape[-1]), preferred_element_type=jnp.float32)
        ret_send[at, rows(s), :] = back.astype(jnp.bfloat16)
        send(kind, s, ret_send.at[at, rows(s)], ret_out.at[at, rows(s)], below)

    def k(s):
        for kind, at in quarters[:3]:
            give_back(kind, s, at)

    def g(s):
        arrive("fw_r", s, amp.at[xo, half(s, 0)], left)
        arrive("fw_l", s, amp.at[xo, half(s, 1)], right)
        if s in split:
            give_back("ret", s, xo)
        else:
            block = amp[:, rows(s), :].reshape(NX * STEPS[s], -1)
            back = jnp.dot(block, mine[...].reshape(-1, mine.shape[-1]), preferred_element_type=jnp.float32)
            ret_send[:, rows(s), :] = back.astype(jnp.bfloat16).reshape(NX, STEPS[s], -1)
            send("ret", s, ret_send.at[:, rows(s), :], ret_out.at[:, rows(s), :], below)

    def q(_):
        virt = NX * amp.shape[1]
        acc[...] = lax.dot_general(
            amp[...].reshape(virt, virt), left_b[...].reshape(virt, -1), (((0,), (0,)), ((), ())),
            preferred_element_type=jnp.float32,
        )

    act = {"h": h, "p": p, "r": r, "z": z, "a": a, "f": f, "k": k, "g": g, "q": q}

    def run(order):
        for item in reversed(order):
            first[item[0]] = int(item[1:])
        for item in order:
            act[item[0]](int(item[1:]))

    run(ORDER)
    store = pltpu.make_async_copy(acc, acc_out, local_sem.at[2])
    store.start()

    for s in range(len(STEPS)):
        if s in split:
            for kind, at in quarters:
                arrive(kind, s, ret_out.at[at, rows(s)], above)
        else:
            arrive("ret", s, ret_out.at[:, rows(s), :], above)
    for (kind, s, _), (src, dst, device, only) in started.items():
        if only is None:
            copy(kind, s, src, dst, device).wait_send()
        else:
            pl.when(only)(copy(kind, s, src, dst, device).wait_send)
    store.wait()


def add(kept_ref, returned_ref, out_ref, total, returned, sem):
    rows = total.shape[0] // ADD_PIECES
    pieces = [pl.ds(i * rows, rows) for i in range(ADD_PIECES)]
    loads = [
        (
            pltpu.make_async_copy(kept_ref.at[at], total.at[at], sem.at[0, i]),
            pltpu.make_async_copy(returned_ref.at[at], returned.at[at], sem.at[1, i]),
        )
        for i, at in enumerate(pieces)
    ]
    for pair in loads:
        for one in pair:
            one.start()
    stores = []
    for i, at in enumerate(pieces):
        for one in loads[i]:
            one.wait()
        total[at, :] += returned[at, :].astype(jnp.float32)
        stores.append(pltpu.make_async_copy(total.at[at], out_ref.at[at], sem.at[2, i]))
        stores[i].start()
    for one in stores:
        one.wait()


def per_device(ints_b, occ_energy, virt_energy):
    _, virt, naux = ints_b.shape
    quarter = virt // NX
    bf16, f32 = jnp.bfloat16, jnp.float32
    steps = len(STEPS)
    hbm, vmem = pl.BlockSpec(memory_space=pltpu.HBM), pl.BlockSpec(memory_space=pltpu.VMEM)
    slab = pltpu.VMEM((quarter, virt), bf16)
    kept, returned = pl.pallas_call(
        kernel,
        out_shape=(jax.ShapeDtypeStruct((virt, naux), f32), jax.ShapeDtypeStruct((NX, quarter, naux), bf16)),
        in_specs=[hbm, pl.BlockSpec(memory_space=pltpu.SMEM), hbm],
        out_specs=(hbm, hbm),
        scratch_shapes=[
            pltpu.VMEM((NX, quarter, naux), bf16),
            pltpu.VMEM((NX, quarter, naux), bf16),
            pltpu.VMEM((NX, quarter, naux), bf16),
            pltpu.VMEM((1, virt), f32),
            pltpu.VMEM((NX, quarter, virt), bf16),
            slab, slab, slab, slab, slab, slab,
            slab, slab,
            pltpu.VMEM((NX, quarter, virt), bf16),
            pltpu.VMEM((quarter, virt), f32),
            pltpu.VMEM((8, virt), f32),
            pltpu.VMEM((8, virt), f32),
            pltpu.VMEM((NX, quarter, naux), bf16),
            pltpu.VMEM((virt, naux), f32),
            pltpu.SemaphoreType.DMA((len(KINDS), steps)),
            pltpu.SemaphoreType.DMA((len(KINDS), steps)),
            pltpu.SemaphoreType.DMA((3,)),
            pltpu.SemaphoreType.REGULAR,
        ],
        compiler_params=pltpu.CompilerParams(collective_id=0, has_side_effects=True, vmem_limit_bytes=56 * 2**20),
        cost_estimate=pl.CostEstimate(flops=6 * virt * virt * naux, bytes_accessed=10 * virt * naux, transcendentals=0),
        name="pair_gradient",
    )(ints_b.reshape(NX, quarter, naux), occ_energy, virt_energy.reshape(1, virt))
    total = pl.pallas_call(
        add,
        out_shape=jax.ShapeDtypeStruct((virt, naux), f32),
        in_specs=[hbm, hbm],
        out_specs=hbm,
        scratch_shapes=[
            pltpu.VMEM((virt, naux), f32),
            pltpu.VMEM((virt, naux), bf16),
            pltpu.SemaphoreType.DMA((3, ADD_PIECES)),
        ],
        compiler_params=pltpu.CompilerParams(vmem_limit_bytes=56 * 2**20),
        name="add_returned",
    )(kept, returned.reshape(virt, naux))
    return total.reshape(1, virt, naux)


def solution(mesh):
    placed = (P("occ", None, "aux"), P("occ"), P())
    return jax.shard_map(
        per_device, mesh=mesh, in_specs=placed, out_specs=P("occ", None, "aux"), check_vma=False
    )
```

```python
import functools

import jax
import jax.numpy as jnp
from jax import lax
from jax.experimental import pallas as pl
from jax.experimental.pallas import tpu as pltpu
from jax.sharding import PartitionSpec as P

MESH = pl.DeviceIdType.MESH
ADD_PIECES = 4
NX = 4
PLANE = 16
STEPS = (64, 64, 64, 32, 32)
RELAYED = (1, 2, 4)
ORDER = ('p0', 'p1', 'e0', 'r0', 'h1', 'p2', 'r1', 'z0', 'h2', 'p3', 'r2', 'z1', 'h4', 'p4', 'r3', 'z2', 'r4', 'z3', 'z4', 'a0', 'a1', 'f0', 'a2', 'f1', 'g0', 'a3', 'f2', 'g1', 'a4', 'f3', 'g2', 'f4', 'g3', 'k4', 'g4', 'q0')
KINDS = (
    "b", "e", "hop", "relay_r", "relay_l", "direct_r", "direct_l", "sum_r", "sum_l", "z", "ag_r", "ag_l", "fw_r", "fw_l", "ret",
    "ret_own", "ret_l", "ret_r",
)


def kernel(
    ints_ref, energy_ref, virt_hbm, acc_out, ret_out,
    mine, left_b, hop, virt_ref, part, relay_l, relay_r, direct_l, direct_r, sum_l, sum_r,
    zsend, zrecv, amp, inverse, esend, erecv, ret_send, acc,
    send_sem, recv_sem, local_sem, late_sem,
):
    occ, aux = lax.axis_index("occ"), lax.axis_index("aux")
    n_occ = lax.axis_size("occ")
    x, zh = lax.rem(aux, NX), aux // NX
    xr, xl, xo = lax.rem(x + 1, NX), lax.rem(x + NX - 1, NX), lax.rem(x + 2, NX)
    right, left = (occ, zh * NX + xr), (occ, zh * NX + xl)
    partner = (occ, (1 - zh) * NX + x)
    above, below = (lax.rem(occ + 1, n_occ), aux), (lax.rem(occ + n_occ - 1, n_occ), aux)
    offsets = [sum(STEPS[:s]) for s in range(len(STEPS))]

    load = pltpu.make_async_copy(ints_ref, mine, local_sem.at[0])
    load.start()
    load_virt = pltpu.make_async_copy(virt_hbm, virt_ref, local_sem.at[1])
    load_virt.start()
    energy = energy_ref[0]
    esend[...] = jnp.full(esend.shape, energy, jnp.float32)

    place = lax.rem(occ, PLANE)
    top = place // (PLANE - 1)
    bottom = 1 - (place + PLANE - 1) // PLANE
    next_top = (lax.rem(occ + PLANE, n_occ), aux)
    last_top = (lax.rem(occ + n_occ - PLANE, n_occ), aux)
    first_here = (lax.rem(occ + n_occ - PLANE + 1, n_occ), aux)
    top_here = (lax.rem(occ + PLANE - 1, n_occ), aux)

    is_top, not_top = top == 1, top == 0

    def greet(device):
        pl.semaphore_signal(barrier, inc=1, device_id=device, device_id_type=MESH)

    barrier = pltpu.get_barrier_semaphore()
    for device in (right, left, above, below):
        greet(device)

    @pl.when(zh == 0)
    def _():
        greet(partner)

    @pl.when(is_top)
    def _():
        greet(next_top)
        greet(last_top)
        greet(first_here)

    @pl.when(bottom == 1)
    def _():
        greet(top_here)

    pl.semaphore_wait(barrier, 4 + zh + 3 * top + bottom)

    @pl.when(zh == 1)
    def _():
        pl.semaphore_signal(late_sem, inc=1, device_id=partner, device_id_type=MESH)

    load.wait()

    started = {}
    first = {}

    def copy(kind, s, src, dst, device):
        at = KINDS.index(kind)
        return pltpu.make_async_remote_copy(
            src_ref=src, dst_ref=dst, send_sem=send_sem.at[at, s], recv_sem=recv_sem.at[at, s],
            device_id=device, device_id_type=MESH,
        )

    def send(kind, s, src, dst, device, only=None):
        one = copy(kind, s, src, dst, device)
        if only is None:
            one.start()
        else:
            pl.when(only)(one.start)
        started[kind, s, only is is_top] = (src, dst, device, only)

    def arrive(kind, s, dst, device):
        copy(kind, s, dst, dst, device).wait_recv()

    def rows(s):
        return pl.ds(offsets[s], STEPS[s])

    def half(s, h):
        return pl.ds(offsets[s] + h * STEPS[s] // 2, STEPS[s] // 2)

    def f32(value):
        return value.astype(jnp.float32)

    send("e", 0, esend, erecv, above)
    for s in range(len(STEPS)):
        if s in RELAYED:
            send("b", s, mine.at[:, rows(s), :], left_b.at[:, rows(s), :], above, not_top)
            send("hop", s, mine.at[:, rows(s), :], hop.at[:, rows(s), :], next_top, is_top)
        else:
            send("b", s, mine.at[:, rows(s), :], left_b.at[:, rows(s), :], above)
    load_virt.wait()

    def prepare(_):
        arrive("e", 0, erecv, below)
        quarter = amp.shape[1]
        column = jnp.broadcast_to(
            virt_ref[0:1, pl.ds(pl.multiple_of(x * quarter, quarter), quarter)], (128, quarter)
        ).T
        row = erecv[0:1, :] + energy - virt_ref[0:1, :]
        inverse[...] = 1.0 / (row - column[:, 0:1])

    def h(s):
        @pl.when(is_top)
        def _():
            arrive("hop", s, hop.at[:, rows(s), :], last_top)

        send("b", s, hop.at[:, rows(s), :], left_b.at[:, rows(s), :], first_here, is_top)

    def p(s):
        arrive("b", s, left_b.at[:, rows(s), :], below)
        theirs = left_b[:, rows(s), :].reshape(NX * STEPS[s], -1)
        value = lax.dot_general(
            theirs, mine[...].reshape(-1, mine.shape[-1]), (((1,), (1,)), ((), ())), preferred_element_type=jnp.float32
        )
        part[:, rows(s), :] = value.astype(jnp.bfloat16).reshape(NX, STEPS[s], -1)
        send("relay_r", s, part.at[xo, half(s, 0)], relay_l.at[half(s, 0)], right)
        send("relay_l", s, part.at[xo, half(s, 1)], relay_r.at[half(s, 1)], left)
        send("direct_r", s, part.at[xr, half(s, 1)], direct_l.at[half(s, 1)], right)
        send("direct_l", s, part.at[xl, half(s, 0)], direct_r.at[half(s, 0)], left)

    def r(s):
        arrive("relay_r", s, relay_l.at[half(s, 0)], left)
        relay_l[half(s, 0), :] = (f32(relay_l[half(s, 0), :]) + f32(part[xr, half(s, 0), :])).astype(jnp.bfloat16)
        send("sum_r", s, relay_l.at[half(s, 0)], sum_l.at[half(s, 0)], right)
        arrive("relay_l", s, relay_r.at[half(s, 1)], right)
        relay_r[half(s, 1), :] = (f32(relay_r[half(s, 1), :]) + f32(part[xl, half(s, 1), :])).astype(jnp.bfloat16)
        send("sum_l", s, relay_r.at[half(s, 1)], sum_r.at[half(s, 1)], left)

    def sum_halves(s):
        arrive("direct_l", s, direct_r.at[half(s, 0)], right)
        arrive("sum_r", s, sum_l.at[half(s, 0)], left)
        zsend[half(s, 0), :] = (
            f32(part[x, half(s, 0), :]) + f32(sum_l[half(s, 0), :]) + f32(direct_r[half(s, 0), :])
        ).astype(jnp.bfloat16)
        arrive("direct_r", s, direct_l.at[half(s, 1)], left)
        arrive("sum_l", s, sum_r.at[half(s, 1)], right)
        zsend[half(s, 1), :] = (
            f32(part[x, half(s, 1), :]) + f32(sum_r[half(s, 1), :]) + f32(direct_l[half(s, 1), :])
        ).astype(jnp.bfloat16)

    def z(s):
        sum_halves(s)
        if s == first["z"]:

            @pl.when(zh == 0)
            def _():
                pl.semaphore_wait(late_sem, 1)

        send("z", s, zsend.at[rows(s)], zrecv.at[rows(s)], partner)

    def a(s):
        arrive("z", s, zrecv.at[rows(s)], partner)
        coulomb = f32(zsend[rows(s), :]) + f32(zrecv[rows(s), :])
        amp[x, rows(s), :] = (coulomb * inverse[rows(s), :]).astype(jnp.bfloat16)
        send("ag_r", s, amp.at[x, rows(s)], amp.at[x, rows(s)], right)
        send("ag_l", s, amp.at[x, rows(s)], amp.at[x, rows(s)], left)

    def f(s):
        arrive("ag_r", s, amp.at[xl, rows(s)], left)
        send("fw_r", s, amp.at[xl, half(s, 0)], amp.at[xl, half(s, 0)], right)
        arrive("ag_l", s, amp.at[xr, rows(s)], right)
        send("fw_l", s, amp.at[xr, half(s, 1)], amp.at[xr, half(s, 1)], left)

    split = [int(item[1:]) for item in ORDER if item[0] == "k"]
    quarters = (("ret_own", x), ("ret_l", xl), ("ret_r", xr), ("ret", xo))

    def give_back(kind, s, at):
        back = jnp.dot(amp[at, rows(s), :], mine[...].reshape(-1, mine.shape[-1]), preferred_element_type=jnp.float32)
        ret_send[at, rows(s), :] = back.astype(jnp.bfloat16)
        send(kind, s, ret_send.at[at, rows(s)], ret_out.at[at, rows(s)], below)

    def k(s):
        for kind, at in quarters[:3]:
            give_back(kind, s, at)

    def g(s):
        arrive("fw_r", s, amp.at[xo, half(s, 0)], left)
        arrive("fw_l", s, amp.at[xo, half(s, 1)], right)
        if s in split:
            give_back("ret", s, xo)
        else:
            block = amp[:, rows(s), :].reshape(NX * STEPS[s], -1)
            back = jnp.dot(block, mine[...].reshape(-1, mine.shape[-1]), preferred_element_type=jnp.float32)
            ret_send[:, rows(s), :] = back.astype(jnp.bfloat16).reshape(NX, STEPS[s], -1)
            send("ret", s, ret_send.at[:, rows(s), :], ret_out.at[:, rows(s), :], below)

    def q(_):
        virt = NX * amp.shape[1]
        acc[...] = lax.dot_general(
            amp[...].reshape(virt, virt), left_b[...].reshape(virt, -1), (((0,), (0,)), ((), ())),
            preferred_element_type=jnp.float32,
        )

    act = {"e": prepare, "h": h, "p": p, "r": r, "z": z, "a": a, "f": f, "k": k, "g": g, "q": q}

    def run(order):
        for item in reversed(order):
            first[item[0]] = int(item[1:])
        for item in order:
            act[item[0]](int(item[1:]))

    run(ORDER)
    store = pltpu.make_async_copy(acc, acc_out, local_sem.at[2])
    store.start()

    for s in range(len(STEPS)):
        if s in split:
            for kind, at in quarters:
                arrive(kind, s, ret_out.at[at, rows(s)], above)
        else:
            arrive("ret", s, ret_out.at[:, rows(s), :], above)
    for (kind, s, _), (src, dst, device, only) in started.items():
        if only is None:
            copy(kind, s, src, dst, device).wait_send()
        else:
            pl.when(only)(copy(kind, s, src, dst, device).wait_send)
    store.wait()


def add(kept_ref, returned_ref, out_ref, total, returned, sem):
    rows = total.shape[0] // ADD_PIECES
    pieces = [pl.ds(i * rows, rows) for i in range(ADD_PIECES)]
    loads = [
        (
            pltpu.make_async_copy(kept_ref.at[at], total.at[at], sem.at[0, i]),
            pltpu.make_async_copy(returned_ref.at[at], returned.at[at], sem.at[1, i]),
        )
        for i, at in enumerate(pieces)
    ]
    for pair in loads:
        for one in pair:
            one.start()
    stores = []
    for i, at in enumerate(pieces):
        for one in loads[i]:
            one.wait()
        total[at, :] += returned[at, :].astype(jnp.float32)
        stores.append(pltpu.make_async_copy(total.at[at], out_ref.at[at], sem.at[2, i]))
        stores[i].start()
    for one in stores:
        one.wait()


def per_device(ints_b, occ_energy, virt_energy):
    _, virt, naux = ints_b.shape
    quarter = virt // NX
    bf16, f32 = jnp.bfloat16, jnp.float32
    steps = len(STEPS)
    hbm, vmem = pl.BlockSpec(memory_space=pltpu.HBM), pl.BlockSpec(memory_space=pltpu.VMEM)
    slab = pltpu.VMEM((quarter, virt), bf16)
    kept, returned = pl.pallas_call(
        kernel,
        out_shape=(jax.ShapeDtypeStruct((virt, naux), f32), jax.ShapeDtypeStruct((NX, quarter, naux), bf16)),
        in_specs=[hbm, pl.BlockSpec(memory_space=pltpu.SMEM), hbm],
        out_specs=(hbm, hbm),
        scratch_shapes=[
            pltpu.VMEM((NX, quarter, naux), bf16),
            pltpu.VMEM((NX, quarter, naux), bf16),
            pltpu.VMEM((NX, quarter, naux), bf16),
            pltpu.VMEM((1, virt), f32),
            pltpu.VMEM((NX, quarter, virt), bf16),
            slab, slab, slab, slab, slab, slab,
            slab, slab,
            pltpu.VMEM((NX, quarter, virt), bf16),
            pltpu.VMEM((quarter, virt), f32),
            pltpu.VMEM((8, virt), f32),
            pltpu.VMEM((8, virt), f32),
            pltpu.VMEM((NX, quarter, naux), bf16),
            pltpu.VMEM((virt, naux), f32),
            pltpu.SemaphoreType.DMA((len(KINDS), steps)),
            pltpu.SemaphoreType.DMA((len(KINDS), steps)),
            pltpu.SemaphoreType.DMA((3,)),
            pltpu.SemaphoreType.REGULAR,
        ],
        compiler_params=pltpu.CompilerParams(collective_id=0, has_side_effects=True, vmem_limit_bytes=56 * 2**20),
        cost_estimate=pl.CostEstimate(flops=6 * virt * virt * naux, bytes_accessed=10 * virt * naux, transcendentals=0),
        name="pair_gradient",
    )(ints_b.reshape(NX, quarter, naux), occ_energy, virt_energy.reshape(1, virt))
    total = pl.pallas_call(
        add,
        out_shape=jax.ShapeDtypeStruct((virt, naux), f32),
        in_specs=[hbm, hbm],
        out_specs=hbm,
        scratch_shapes=[
            pltpu.VMEM((virt, naux), f32),
            pltpu.VMEM((virt, naux), bf16),
            pltpu.SemaphoreType.DMA((3, ADD_PIECES)),
        ],
        compiler_params=pltpu.CompilerParams(vmem_limit_bytes=56 * 2**20),
        name="add_returned",
    )(kept, returned.reshape(virt, naux))
    return total.reshape(1, virt, naux)


def solution(mesh):
    placed = (P("occ", None, "aux"), P("occ"), P())
    return jax.shard_map(
        per_device, mesh=mesh, in_specs=placed, out_specs=P("occ", None, "aux"), check_vma=False
    )
```
